256 devices in a mesh: group: 32 (over z, x), tensor: 8 (over y, core).
Axes of the slice: x: 4, y: 4, z: 8, core: 2. Of those that a mesh axis runs over, the one named last changes fastest.
Arguments:
- queries: bfloat16 [8192, 8192], P('group', 'tensor'), may hold values from -200 to 200
- rotated_keys: bfloat16 [8192, 1024], P('group', 'tensor'), may hold values from -8 to 8
- value_rows_all: bfloat16 [8192, 1024], P('group', 'tensor'), may hold values from -6 to 6
- output_weight: bfloat16 [8192, 8192], P('tensor', 'group'), may hold values from -0.0625 to 0.0625
- adapter_down: bfloat16 [32, 8192, 64], P('group', 'tensor'), may hold values from -0.0625 to 0.0625
- adapter_up: bfloat16 [32, 64, 8192], P(None, None, 'tensor'), may hold values from -0.75 to 0.75
- tenant_of_block: int32 [64], P('group'), may hold values from 0 to 31
- tenant_page_slots: int32 [32], replicated, may hold values from 0 to 31, each once
- prefix_length: int32 [32], replicated, may hold values from 1 to 256
Outputs:
- mixed: bfloat16 [8192, 8192], P('group', 'tensor')
The draws below stay inside these ranges and needn't reach their ends.
Inputs may be any that keep to these rules, and one draw needn't show every extreme that they name: `tenant_page_slots`: each page slot is used by exactly one tenant.
All inputs are finite; a program needn't handle non-finite values.
Results may differ from the reference program's by a relative error of at most 0.023.
Values may be sent and summed in bfloat16 or wider, within the bound.
A program may use at most 128 MiB of HBM per device.

```python
import math
import jax
import jax.numpy as jnp
import numpy as np
from jax import lax

MODEL_WIDTH = 8192
HEADS = 64
KV_HEADS = 8
HEAD_DIM = 128
ADAPTER_RANK = 64
BLOCK_SIZE = 128
NB = 2
QUERY_WIDTH = 8192
ROWS = 256
TOKEN_COUNT = 8192
TENANT_SLOTS = 32
N_GROUP = 32
N_TENSOR = 8


def base_keys(key):
    return jnp.clip(jax.random.normal(key, (TOKEN_COUNT, KV_HEADS * HEAD_DIM), jnp.float32), -6.0, 6.0)


def draw_rotated_keys(key, part):
    states = base_keys(key)
    return states.astype(jnp.bfloat16)


def draw_queries(key, part):
    key = jax.random.fold_in(key, 7)
    values = jnp.clip(jax.random.normal(key, (TOKEN_COUNT, HEADS * HEAD_DIM), jnp.float32), -6.0, 6.0)
    return values.astype(jnp.bfloat16)


def place_ends(drawn, rng, smallest, largest):
    shape = drawn.shape
    index_at = [jax.random.randint(jax.random.fold_in(rng, axis), (), 0, shape[axis]) for axis in range(len(shape))]
    drawn = drawn.at[tuple(index_at)].set(smallest)
    longest = shape.index(max(shape))
    index_at[longest] = (index_at[longest] + 1) % shape[longest]
    return drawn.at[tuple(index_at)].set(largest)


def steps_of(key, dims, cuts, smallest, largest):
    level = 1.0
    for axis_at, parts in cuts:
        heights = jax.random.uniform(jax.random.fold_in(jax.random.fold_in(key, 6), axis_at), (parts,), jnp.float32, smallest / len(cuts), largest / len(cuts))
        level = level * jnp.repeat(jnp.exp(heights), dims[axis_at] // parts).reshape((-1,) + (1,) * (len(dims) - 1 - axis_at))
    return level


def cumulative_ranks(number_of, slope):
    weights = [(1 << 20) // math.isqrt(grade ** slope) + 1 for grade in range(1, number_of + 1)]
    scale = 1 + sum(weights) // (1 << 30)
    return np.cumsum(np.array([max(1, weight // scale) for weight in weights]))


def ranked_ids(rng, dims, number_of, slope):
    table = cumulative_ranks(number_of, slope)
    pick = jax.random.randint(jax.random.fold_in(rng, 1), dims, 0, int(table[number_of - 1]))
    rank = jnp.searchsorted(jnp.asarray(table, jnp.int32), pick, side="right")
    return jax.random.permutation(jax.random.fold_in(rng, 2), number_of)[rank].astype(jnp.int32)


def gaussian(rng, dims, scale, most, split=(), dtype=jnp.bfloat16):
    values = jax.random.normal(rng, dims, jnp.float32) * scale
    if len(split) > 0:
        values = steps_of(rng, dims, split, -0.22, 0.18) * values
    return jnp.clip(values, min=-most, max=most).astype(dtype)


def setup_inputs(seed: int = 0) -> dict:
    key_list = jax.random.split(jax.random.key(seed), 10)
    queries = draw_queries(jax.random.fold_in(key_list[9], 71), 0)
    rotated_keys = draw_rotated_keys(jax.random.fold_in(key_list[9], 71), 0)
    value_rows_all = gaussian(key_list[2], (TOKEN_COUNT, KV_HEADS * HEAD_DIM), 2.0, 6.0, ((0, 32), (1, 8)))
    output_weight = gaussian(key_list[3], (QUERY_WIDTH, MODEL_WIDTH), QUERY_WIDTH ** -0.5, 0.0625, ((0, 8), (1, 32)))
    adapter_down = gaussian(key_list[4], (TENANT_SLOTS, QUERY_WIDTH, ADAPTER_RANK), QUERY_WIDTH ** -0.5, 0.0625, ((0, 32), (1, 8)))
    adapter_up = gaussian(key_list[5], (TENANT_SLOTS, ADAPTER_RANK, MODEL_WIDTH), ADAPTER_RANK ** -0.5, 0.75, ((2, 8),))
    tenant_of_block = place_ends(ranked_ids(key_list[6], (TOKEN_COUNT // BLOCK_SIZE,), TENANT_SLOTS, 2), jax.random.fold_in(key_list[6], 3), 0, TENANT_SLOTS - 1).astype(jnp.int32)
    tenant_page_slots = jax.random.permutation(key_list[7], TENANT_SLOTS).astype(jnp.int32)
    prefix_length = place_ends(jax.random.randint(key_list[8], (TENANT_SLOTS,), 1, NB * BLOCK_SIZE + 1), jax.random.fold_in(key_list[8], 1), 1, NB * BLOCK_SIZE).astype(jnp.int32)
    return {"queries": queries, "rotated_keys": rotated_keys, "value_rows_all": value_rows_all, "output_weight": output_weight, "adapter_down": adapter_down, "adapter_up": adapter_up, "tenant_of_block": tenant_of_block, "tenant_page_slots": tenant_page_slots, "prefix_length": prefix_length}


def layout(tenants, prefix_length):
    block_index = jnp.arange(NB)
    same_tenant = tenants[:, None] == tenants[None, :]
    earlier = jnp.sum((same_tenant & (block_index[None, :] < block_index[:, None])).astype(jnp.int32), axis=1)
    row_tenant = jnp.repeat(tenants, BLOCK_SIZE)
    position = jnp.repeat(earlier, BLOCK_SIZE) * BLOCK_SIZE + jnp.tile(jnp.arange(BLOCK_SIZE), NB)
    matches = row_tenant[:, None] == jnp.arange(TENANT_SLOTS)[None, :]
    length = jnp.sum(jnp.where(matches, prefix_length[None, :], 0), axis=1)
    row_validity = position < length
    row_index = jnp.arange(NB * BLOCK_SIZE)
    visible = (row_tenant[:, None] == row_tenant[None, :]) & (row_index[None, :] <= row_index[:, None]) & row_validity[None, :]
    return visible, row_validity


def attend(query_rows, key_rows, value_rows, visible):
    groups = HEADS // KV_HEADS
    block_count = query_rows.shape[0]
    qfull = query_rows.astype(jnp.float32).reshape(block_count, KV_HEADS, groups, HEAD_DIM)
    kfull = key_rows.astype(jnp.float32).reshape(block_count, KV_HEADS, HEAD_DIM)
    vfull = value_rows.astype(jnp.float32).reshape(block_count, KV_HEADS, HEAD_DIM)
    scores = jnp.einsum('rkgd,skd->kgrs', qfull, kfull) * (HEAD_DIM ** -0.5)
    scores = jnp.where(visible[None, None], scores, -jnp.inf)
    peak = jnp.max(scores, axis=-1, keepdims=True)
    expo = jnp.exp(scores - peak)
    probs = (expo / jnp.sum(expo, axis=-1, keepdims=True)).astype(jnp.bfloat16)
    mixed_heads = jnp.einsum('kgrs,skd->rkgd', probs.astype(jnp.float32), vfull)
    return mixed_heads.reshape(block_count, HEADS * HEAD_DIM).astype(jnp.bfloat16)


def reference(queries, rotated_keys, value_rows_all, output_weight, adapter_down, adapter_up, tenant_of_block, tenant_page_slots, prefix_length):
    feature_width = HEADS * HEAD_DIM
    kwidth = KV_HEADS * HEAD_DIM

    def per_group(inputs):
        query_rows, key_rows, value_rows, tenants = inputs
        visible, row_validity = layout(tenants, prefix_length)
        return attend(query_rows, key_rows, value_rows, visible), row_validity

    head_result, row_validity = lax.map(per_group, (queries.reshape(N_GROUP, ROWS, feature_width), rotated_keys.reshape(N_GROUP, ROWS, kwidth), value_rows_all.reshape(N_GROUP, ROWS, kwidth), tenant_of_block.reshape(N_GROUP, NB)))
    head_result = head_result.reshape(TOKEN_COUNT, feature_width)
    row_validity = row_validity.reshape(TOKEN_COUNT)
    share = feature_width // N_TENSOR
    base_output = jnp.zeros((TOKEN_COUNT, MODEL_WIDTH), jnp.float32)
    for slice_index in range(N_TENSOR):
        partial_value = jnp.dot(head_result[:, slice_index * share:(slice_index + 1) * share], output_weight[slice_index * share:(slice_index + 1) * share], preferred_element_type=jnp.float32)
        base_output = base_output + lax.optimization_barrier(partial_value.astype(jnp.bfloat16)).astype(jnp.float32)
    page_slots = tenant_page_slots[tenant_of_block].astype(jnp.int32)

    def block_values(inputs):
        rows_per_block, page_slot = inputs
        down_projected = jnp.dot(rows_per_block, adapter_down[page_slot], preferred_element_type=jnp.float32).astype(jnp.bfloat16)
        return jnp.dot(down_projected, adapter_up[page_slot], preferred_element_type=jnp.float32)

    adapter_output = lax.map(block_values, (head_result.reshape(TOKEN_COUNT // BLOCK_SIZE, BLOCK_SIZE, feature_width), page_slots)).reshape(TOKEN_COUNT, MODEL_WIDTH)
    return jnp.where(row_validity[:, None], base_output + adapter_output, 0.0).astype(jnp.bfloat16)
```

```python
import functools

import jax
import jax.numpy as jnp
from jax import lax
from jax.experimental import pallas as pl
from jax.experimental.pallas import tpu as pltpu
from jax.sharding import PartitionSpec as P

MESH = pl.DeviceIdType.MESH
HEADS = 8
DIM = 128
BLOCK = 128
NZ, NX, NY, NT = 8, 4, 4, 8
WIDTH = 1024
STEPS = 8
LAST = 7
EXP2_SCALE = DIM ** (-0.5) * 1.4426950408889634
F32 = jnp.float32
BF16 = jnp.bfloat16


def matmul(a, b):
    return jnp.dot(a, b, preferred_element_type=F32)


def matmul_t(a, b):
    return lax.dot_general(a, b, (((1,), (1,)), ((), ())), preferred_element_type=F32)


def kernel(
    q_hbm, k_hbm, v_hbm, w_hbm, down_hbm, up_hbm, tenant_ref, slot_ref, length_ref,
    out_ref,
    qv, kv, vv, hbuf, slots, wbuf, pbuf, upv,
    psend, prec, own, rsend, rrec, fsend, fin, acc,
    asend, arec, tsend, trec,
    lsem, wss, wrs, pss, prs, hss, hrs, sss, srs, pxs, pxr, rss, rrs, fss, frs,
    axs, axr, ats, atr,
):
    g, t = lax.axis_index("group"), lax.axis_index("tensor")
    z, x = g // NX, g % NX
    y, c = t // 2, t % 2
    z_next = ((z + 1) % NZ) * NX + x
    z_prev = ((z + NZ - 1) % NZ) * NX + x

    barrier = pltpu.get_barrier_semaphore()
    for peer in (z_next, z_prev):
        pl.semaphore_signal(barrier, inc=1, device_id=(peer, t), device_id_type=MESH)

    def greet(d, carry):
        peer = (x * NT + t + d) % (NX * NT)
        pl.semaphore_signal(
            barrier, inc=1, device_id=(z * NX + peer // NT, peer % NT), device_id_type=MESH
        )
        return carry

    lax.fori_loop(1, NX * NT, greet, 0)
    pl.semaphore_wait(barrier, NX * NT + 1)

    def remote(src, dst, ssem, rsem, device):
        return pltpu.make_async_remote_copy(
            src_ref=src, dst_ref=dst, send_sem=ssem, recv_sem=rsem,
            device_id=device, device_id_type=MESH,
        )

    def item(d, s):
        half = s % 2 if d == 0 else 1 - s % 2
        tile = (z + NZ - s // 2) % NZ if d == 0 else (z + s // 2) % NZ
        return tile, half

    def w_copy(d, s, first=False):
        tile, half = item(d, s)
        src = w_hbm.at[:, half * 128 : half * 128 + 128] if first else wbuf.at[tile, half]
        return remote(
            src, wbuf.at[tile, half], wss.at[d, s], wrs.at[d, s],
            (z_next if d == 0 else z_prev, t),
        )

    def p_copy(d, s, first=False):
        tile, half = item(d, s)
        src = down_hbm.at[half * 32 : half * 32 + 32, :] if first else pbuf.at[tile, half]
        return remote(
            src, pbuf.at[tile, half], pss.at[d, s], prs.at[d, s],
            (z_next if d == 0 else z_prev, t),
        )

    for make in (p_copy, w_copy):
        for s in range(2):
            for d in range(2):
                make(d, s, True).start()

    def arrived(make, j):
        for d in range(2):
            make(d, j - 1).wait_recv()
            if j + 1 < LAST:
                make(d, j + 1).start()

    q_in = pltpu.make_async_copy(q_hbm, qv, lsem.at[0])
    k_in = pltpu.make_async_copy(k_hbm, kv, lsem.at[1])
    v_in = pltpu.make_async_copy(v_hbm, vv, lsem.at[2])
    w_in = [
        pltpu.make_async_copy(w_hbm.at[:, h * 128 : h * 128 + 128], wbuf.at[z, h], lsem.at[3 + h])
        for h in range(2)
    ]
    d_in = [
        pltpu.make_async_copy(down_hbm.at[h * 32 : h * 32 + 32, :], pbuf.at[z, h], lsem.at[5 + h])
        for h in range(2)
    ]
    up_in = pltpu.make_async_copy(up_hbm, upv, lsem.at[7])
    local = [k_in, q_in, v_in] + w_in + d_in + [up_in]
    for copy in local:
        copy.start()

    tenant0, tenant1 = tenant_ref[0], tenant_ref[1]
    same = tenant0 == tenant1
    length0, length1 = length_ref[tenant0], length_ref[tenant1]
    slot0, slot1 = slot_ref[tenant0], slot_ref[tenant1]
    shift1 = jnp.where(same, BLOCK, 0)
    reach0 = jnp.where(same, length0, 0)

    rows8 = lax.broadcasted_iota(jnp.int32, (8, 128), 0)
    slots[x] = jnp.where(rows8 == 0, slot0, slot1).astype(F32)

    def slot_copy(d):
        return remote(
            slots.at[x], slots.at[x], sss.at[d - 1], srs.at[d - 1], (z * NX + (x + d) % NX, t)
        )

    for d in range(1, NX):
        slot_copy(d).start()

    def h_copy(d, i):
        if i < 2:
            b, tile = i, x
        else:
            b, tile = d, (x + NX - 1) % NX if d == 0 else (x + 1) % NX
        at = hbuf.at[b, pl.ds(pl.multiple_of(tile * BLOCK, BLOCK), BLOCK), :]
        to = (x + 1) % NX if d == 0 else (x + NX - 1) % NX
        return remote(at, at, hss.at[d, i], hrs.at[d, i], (z * NX + to, t))

    k_in.wait()
    q_in.wait()
    v_in.wait()
    row = lax.broadcasted_iota(jnp.int32, (BLOCK, BLOCK), 0)
    col = lax.broadcasted_iota(jnp.int32, (BLOCK, BLOCK), 1)
    causal = col <= row
    masks = (
        [causal & (col < length0)],
        [col < reach0, causal & (col + shift1 < length1)],
    )
    here = pl.ds(pl.multiple_of(x * BLOCK, BLOCK), BLOCK)
    for b in range(2):
        keys = [kv[j * BLOCK : (j + 1) * BLOCK, :] for j in range(b + 1)]
        values = [vv[j * BLOCK : (j + 1) * BLOCK, :] for j in range(b + 1)]
        for h in range(HEADS):
            query = qv[b * BLOCK : (b + 1) * BLOCK, h * DIM : (h + 1) * DIM]
            scores = [
                jnp.where(mask, matmul_t(query, key), -1e30)
                for mask, key in zip(masks[b], keys)
            ]
            peak = functools.reduce(
                jnp.maximum, [jnp.max(s, axis=1, keepdims=True) for s in scores]
            )
            expo = [jnp.exp2((s - peak) * EXP2_SCALE) for s in scores]
            total = functools.reduce(
                jnp.add, [jnp.sum(e, axis=1, keepdims=True) for e in expo]
            )
            inverse = 1.0 / total
            mixed = functools.reduce(
                jnp.add,
                [matmul((e * inverse).astype(BF16), value) for e, value in zip(expo, values)],
            )
            hbuf[b, here, h * DIM : (h + 1) * DIM] = mixed.astype(BF16)
        for d in range(2):
            h_copy(d, b).start()

    arrived(p_copy, 1)
    arrived(p_copy, 2)
    arrived(w_copy, 1)
    arrived(p_copy, 3)
    h_copy(0, 0).wait_recv()
    h_copy(0, 2).start()
    arrived(p_copy, 4)
    arrived(w_copy, 2)
    arrived(p_copy, 5)
    h_copy(1, 1).wait_recv()
    h_copy(1, 2).start()
    arrived(p_copy, 6)
    for d, i in ((0, 1), (1, 0), (0, 2), (1, 2)):
        h_copy(d, i).wait_recv()
    arrived(p_copy, 7)
    for copy in w_in + d_in + [up_in]:
        copy.wait()
    for d in range(1, NX):
        slot_copy(d).wait_recv()

    def tiles_of(k):
        off, half = (k + 1) // 2, (k + 1) % 2
        return ((z + NZ - off) % NZ, half), ((z + off) % NZ, 1 - half)

    def pair_copy(k):
        return remote(psend.at[k], prec.at[k], pxs.at[k], pxr.at[k], (g, 2 * y + 1 - c))

    def sum_copy(k, d):
        to = (y + d) % NY
        return remote(
            rsend.at[k, to], rrec.at[k, d - 1], rss.at[k, d - 1], rrs.at[k, d - 1], (g, 2 * to + c)
        )

    def fin_copy(k, i):
        tile, half = tiles_of(k)[i]
        return remote(
            fsend.at[k, i],
            fin.at[x, half, pl.ds(pl.multiple_of(c * BLOCK, BLOCK), BLOCK), :],
            fss.at[k, i], frs.at[x, half, c], (z * NX + y, tile),
        )

    def stays(tile):
        return (x == y) & (tile == t)

    def finish(k):
        part = rsend[k, y].astype(F32)
        for d in range(1, NY):
            sum_copy(k, d).wait_recv()
            part = part + rrec[k, d - 1].astype(F32)
        part = part.astype(BF16)
        for i, (tile, half) in enumerate(tiles_of(k)):
            piece = part[:, i * 128 : (i + 1) * 128]

            @pl.when(stays(tile))
            def _():
                fin[x, half, pl.ds(pl.multiple_of(c * BLOCK, BLOCK), BLOCK), :] = piece

            @pl.when(jnp.logical_not(stays(tile)))
            def _():
                fsend[k, i] = piece
                fin_copy(k, i).start()

    def shrink_copy(d):
        return remote(
            asend.at[(x + d) % NX], arec.at[d - 1], axs.at[d - 1], axr.at[d - 1],
            (z * NX + (x + d) % NX, t),
        )

    def tensor_copy(d):
        return remote(tsend, trec.at[d - 1], ats.at[d - 1], atr.at[d - 1], (g, (t + d) % NT))

    def shrink():
        pages = pbuf[...].reshape(NZ * 64, WIDTH)
        lane = lax.broadcasted_iota(jnp.int32, (1, NZ * 64), 1)
        page = ((lane // 64) * NX + x).astype(F32)
        at = lax.broadcasted_iota(jnp.int32, (NZ * 64, 128), 0) % 64
        to = lax.broadcasted_iota(jnp.int32, (NZ * 64, 128), 1)
        for i in range(NX):
            total = jnp.zeros((BLOCK, 128), F32)
            for b in range(2):
                rows = matmul_t(hbuf[b, i * BLOCK : (i + 1) * BLOCK, :], pages)
                slot = jnp.concatenate([slots[i, b : b + 1, :]] * (NZ * 64 // 128), axis=1)
                rows = jnp.where(slot == page, rows, 0.0).astype(BF16)
                total = total + matmul(rows, (to == at + 64 * b).astype(BF16))
            asend[i] = total.astype(BF16)
        for d in range(1, NX):
            shrink_copy(d).start()

    def shrink_x():
        total = asend[x].astype(F32)
        for d in range(1, NX):
            shrink_copy(d).wait_recv()
            total = total + arec[d - 1].astype(F32)
        tsend[...] = total.astype(BF16)
        for d in range(1, NT):
            tensor_copy(d).start()

    def expand():
        total = tsend[...].astype(F32)
        for d in range(1, NT):
            tensor_copy(d).wait_recv()
            total = total + trec[d - 1].astype(F32)
        shrunk = total.astype(BF16)
        lane = lax.broadcasted_iota(jnp.int32, (BLOCK, 128), 1)
        for b, slot in enumerate((slot0, slot1)):
            acc[b * BLOCK : (b + 1) * BLOCK, :] = matmul(
                jnp.where(lane // 64 == b, shrunk, jnp.zeros_like(shrunk)),
                jnp.concatenate([upv[slot], upv[slot]], axis=0),
            )

    def step(k, carry):
        @pl.when((k == 2) | (k >= 4))
        def _():
            j = jnp.where(k == 2, 3, k)
            for d in range(2):
                w_copy(d, j - 1).wait_recv()

            @pl.when(j + 1 < LAST)
            def _():
                for d in range(2):
                    w_copy(d, j + 1).start()

        (tile_r, half_r), (tile_l, half_l) = tiles_of(k)
        weights = jnp.concatenate([wbuf[tile_r, half_r], wbuf[tile_l, half_l]], axis=1)
        psend[k] = matmul(hbuf[1 - c], weights).astype(BF16)
        pair_copy(k).start()
        own[...] = matmul(hbuf[c], weights)

        @pl.when(k == 1)
        def _():
            shrink()

        @pl.when(k == 3)
        def _():
            shrink_x()

        @pl.when(k == 4)
        def _():
            expand()

        @pl.when(k > 0)
        def _():
            finish(k - 1)

        pair_copy(k).wait_recv()
        total = (own[...] + prec[k].astype(F32)).astype(BF16)
        for i in range(NY):
            rsend[k, i] = total[i * BLOCK : (i + 1) * BLOCK, :]
        for d in range(1, NY):
            sum_copy(k, d).start()
        return carry

    lax.fori_loop(0, STEPS, step, 0)
    finish(STEPS - 1)

    def sent(s, carry):
        for d in range(2):
            p_copy(d, s).wait_send()
            w_copy(d, s).wait_send()
        return carry

    lax.fori_loop(0, LAST, sent, 0)
    for d in range(2):
        for i in range(3):
            h_copy(d, i).wait_send()
    for d in range(1, NX):
        slot_copy(d).wait_send()
        shrink_copy(d).wait_send()
    for d in range(1, NT):
        tensor_copy(d).wait_send()

    def stepped(k, carry):
        pair_copy(k).wait_send()
        for d in range(1, NY):
            sum_copy(k, d).wait_send()
        for i, (tile, _) in enumerate(tiles_of(k)):

            @pl.when(jnp.logical_not(stays(tile)))
            def _():
                fin_copy(k, i).wait_send()

        return carry

    lax.fori_loop(0, STEPS, stepped, 0)

    for i in range(NX):
        for cc in range(2):
            mine = (x == i) & (t == 2 * x + cc)
            for half in range(2):

                @pl.when(jnp.logical_not(mine))
                def _():
                    at = fin.at[i, half, cc * BLOCK : (cc + 1) * BLOCK, :]
                    remote(at, at, fss.at[0, 0], frs.at[i, half, cc], (z_next, t)).wait_recv()

    position = lax.broadcasted_iota(jnp.int32, (BLOCK, 128), 0)
    valid = (position < length0, position + shift1 < length1)
    for b in range(2):
        for i in range(NX):
            for half in range(2):
                cols = slice(i * 256 + half * 128, i * 256 + half * 128 + 128)
                base = fin[i, half, b * BLOCK : (b + 1) * BLOCK, :].astype(F32)
                value = base + acc[b * BLOCK : (b + 1) * BLOCK, cols]
                out_ref[b * BLOCK : (b + 1) * BLOCK, cols] = jnp.where(
                    valid[b], value, 0.0
                ).astype(BF16)


def per_device(q, k, v, w, down, up, tenants, page_slots, lengths):
    dma = pltpu.SemaphoreType.DMA
    anywhere = pl.BlockSpec(memory_space=pl.ANY)
    scalars = pl.BlockSpec(memory_space=pltpu.SMEM)
    rows = 2 * BLOCK
    return pl.pallas_call(
        kernel,
        out_shape=jax.ShapeDtypeStruct((rows, WIDTH), BF16),
        in_specs=[anywhere] * 6 + [scalars] * 3,
        out_specs=pl.BlockSpec(memory_space=pltpu.VMEM),
        scratch_shapes=[
            pltpu.VMEM((rows, WIDTH), BF16),
            pltpu.VMEM((rows, DIM), BF16),
            pltpu.VMEM((rows, DIM), BF16),
            pltpu.VMEM((2, NX * BLOCK, WIDTH), BF16),
            pltpu.VMEM((NX, 8, 128), F32),
            pltpu.VMEM((NZ, 2, WIDTH, 128), BF16),
            pltpu.VMEM((NZ, 2, 32, WIDTH), BF16),
            pltpu.VMEM((32, 64, WIDTH), BF16),
            pltpu.VMEM((STEPS, NX * BLOCK, 256), BF16),
            pltpu.VMEM((STEPS, NX * BLOCK, 256), BF16),
            pltpu.VMEM((NX * BLOCK, 256), F32),
            pltpu.VMEM((STEPS, NY, BLOCK, 256), BF16),
            pltpu.VMEM((STEPS, NY - 1, BLOCK, 256), BF16),
            pltpu.VMEM((STEPS, 2, BLOCK, 128), BF16),
            pltpu.VMEM((NX, 2, rows, 128), BF16),
            pltpu.VMEM((rows, WIDTH), F32),
            pltpu.VMEM((NX, BLOCK, 128), BF16),
            pltpu.VMEM((NX - 1, BLOCK, 128), BF16),
            pltpu.VMEM((BLOCK, 128), BF16),
            pltpu.VMEM((NT - 1, BLOCK, 128), BF16),
            dma((8,)),
            dma((2, LAST)), dma((2, LAST)), dma((2, LAST)), dma((2, LAST)),
            dma((2, 3)), dma((2, 3)),
            dma((NX - 1,)), dma((NX - 1,)),
            dma((STEPS,)), dma((STEPS,)),
            dma((STEPS, NY - 1)), dma((STEPS, NY - 1)),
            dma((STEPS, 2)), dma((NX, 2, 2)),
            dma((NX - 1,)), dma((NX - 1,)),
            dma((NT - 1,)), dma((NT - 1,)),
        ],
        compiler_params=pltpu.CompilerParams(
            collective_id=0, has_side_effects=True, vmem_limit_bytes=56 << 20
        ),
    )(q, k, v, w, jnp.swapaxes(down[0], 0, 1), up, tenants, page_slots, lengths)


def solution(mesh):
    placed = (
        P("group", "tensor"),
        P("group", "tensor"),
        P("group", "tensor"),
        P("tensor", "group"),
        P("group", "tensor", None),
        P(None, None, "tensor"),
        P("group"),
        P(),
        P(),
    )
    return jax.shard_map(
        per_device, mesh=mesh, in_specs=placed, out_specs=P("group", "tensor"), check_vma=False
    )
```

```python
import functools

import jax
import jax.numpy as jnp
from jax import lax
from jax.experimental import pallas as pl
from jax.experimental.pallas import tpu as pltpu
from jax.sharding import PartitionSpec as P

MESH = pl.DeviceIdType.MESH
HEADS = 8
DIM = 128
BLOCK = 128
NZ, NX, NY, NT = 8, 4, 4, 8
WIDTH = 1024
LAST = 7
GROUPS = ((0, 1), (1, 2), (3, 2), (5, 1), (6, 1), (7, 1))
ORDER = (
    "m0", "m1", "w4", "m2", "q0", "q1", "f0", "w5", "m3", "q2", "f1", "p6",
    "p7", "s0", "q3", "f2", "w6", "m4", "x0", "f3", "q4", "w7", "m5", "f4",
    "e0", "q5", "f5",
)
EXP2_SCALE = DIM ** (-0.5) * 1.4426950408889634
F32 = jnp.float32
BF16 = jnp.bfloat16


def matmul(a, b):
    return jnp.dot(a, b, preferred_element_type=F32)


def matmul_t(a, b):
    return lax.dot_general(a, b, (((1,), (1,)), ((), ())), preferred_element_type=F32)


def kernel(
    q_hbm, k_hbm, v_hbm, w_hbm, down_hbm, up_hbm, tenant_ref, slot_ref, length_ref,
    out_ref,
    qv, kv, vv, hbuf, slots, wbuf, pbuf, upv,
    kept, hsend, hrec, qsend, qrec, fsend, fin, acc,
    asend, arec, tsend, trec,
    lsem, wfs, wfr, wss, wrs, pfs, pfr, pss, prs, wps, wpr, hss, hrs, hps, hpr, sss, srs,
    hfs, hfr, qfs, qfr, fss, frs, axs, axr, ats, atr,
):
    g, t = lax.axis_index("group"), lax.axis_index("tensor")
    z, x = g // NX, g % NX
    y, c = t // 2, t % 2
    z_next = ((z + 1) % NZ) * NX + x
    z_prev = ((z + NZ - 1) % NZ) * NX + x
    sibling = (g, 2 * y + 1 - c)
    onward = (z_next * (1 - c) + z_prev * c, t)

    barrier = pltpu.get_barrier_semaphore()
    for peer in (z_next, z_prev):
        for core in range(2):
            pl.semaphore_signal(
                barrier, inc=1, device_id=(peer, 2 * y + core), device_id_type=MESH
            )

    def greet(d, carry):
        peer = (x * NT + t + d) % (NX * NT)
        pl.semaphore_signal(
            barrier, inc=1, device_id=(z * NX + peer // NT, peer % NT), device_id_type=MESH
        )
        return carry

    lax.fori_loop(1, NX * NT, greet, 0)
    pl.semaphore_wait(barrier, NX * NT + 3)

    def remote(src, dst, ssem, rsem, device):
        return pltpu.make_async_remote_copy(
            src_ref=src, dst_ref=dst, send_sem=ssem, recv_sem=rsem,
            device_id=device, device_id_type=MESH,
        )

    def place(k, core):
        off = (k + 1) // 2
        return (z + off * (NZ - 1 + 2 * core)) % NZ, ((k + 1) % 2 + core) % 2

    def w_first(core, s):
        half = s % 2 if core == 0 else 1 - s % 2
        return remote(
            w_hbm.at[:, half * 128 : half * 128 + 128], wbuf.at[s + 1, c],
            wfs.at[core, s], wfr.at[s, c], (z_next if core == 0 else z_prev, 2 * y + core),
        )

    def p_first(core, s):
        half = s % 2 if core == 0 else 1 - s % 2
        return remote(
            down_hbm.at[half * 32 : half * 32 + 32, :], pbuf.at[s + 1, c],
            pfs.at[core, s], pfr.at[s, c], (z_next if core == 0 else z_prev, 2 * y + core),
        )

    def w_copy(s):
        return remote(wbuf.at[s - 1], wbuf.at[s + 1], wss.at[s], wrs.at[s], onward)

    def p_copy(s):
        return remote(pbuf.at[s - 1], pbuf.at[s + 1], pss.at[s], prs.at[s], onward)

    for s in range(2):
        for make in (p_first, w_first):
            for core in range(2):
                make(core, s).start()

    def arrived(buf, fr, make, j):
        if j <= 2:
            for core in range(2):
                at = buf.at[j, core]
                remote(at, at, wss.at[0], fr.at[j - 1, core], onward).wait_recv()
        else:
            make(j - 1).wait_recv()
        if j + 1 < LAST:
            make(j + 1).start()

    w_arrived = functools.partial(arrived, wbuf, wfr, w_copy)
    p_arrived = functools.partial(arrived, pbuf, pfr, p_copy)

    def halves(ref, at):
        return ref.at[:, pl.ds(pl.multiple_of(at * 128, 128), 128)]

    w_pair = remote(halves(w_hbm, c), wbuf.at[0, c], wps.at[0], wpr.at[0], sibling)
    p_pair = remote(
        down_hbm.at[pl.ds(pl.multiple_of(c * 32, 32), 32), :], pbuf.at[0, c],
        wps.at[1], wpr.at[1], sibling,
    )
    q_in = pltpu.make_async_copy(q_hbm, qv, lsem.at[0])
    k_in = pltpu.make_async_copy(k_hbm, kv, lsem.at[1])
    v_in = pltpu.make_async_copy(v_hbm, vv, lsem.at[2])
    w_in = pltpu.make_async_copy(halves(w_hbm, 1 - c), wbuf.at[0, c], lsem.at[3])
    d_in = pltpu.make_async_copy(
        down_hbm.at[pl.ds(pl.multiple_of((1 - c) * 32, 32), 32), :], pbuf.at[0, c], lsem.at[4]
    )
    up_in = pltpu.make_async_copy(up_hbm, upv, lsem.at[5])
    for copy in (k_in, q_in, v_in, w_in, d_in, up_in):
        copy.start()

    tenant0, tenant1 = tenant_ref[0], tenant_ref[1]
    same = tenant0 == tenant1
    length0, length1 = length_ref[tenant0], length_ref[tenant1]
    slot0, slot1 = slot_ref[tenant0], slot_ref[tenant1]
    shift1 = jnp.where(same, BLOCK, 0)
    reach0 = jnp.where(same, length0, 0)

    rows8 = lax.broadcasted_iota(jnp.int32, (8, 128), 0)
    slots[x] = jnp.where(rows8 == 0, slot0, slot1).astype(F32)

    def slot_copy(d):
        return remote(
            slots.at[x], slots.at[x], sss.at[d - 1], srs.at[d - 1], (z * NX + (x + d) % NX, t)
        )

    def piece(core, tile, b):
        return hbuf.at[core, tile, b * BLOCK : (b + 1) * BLOCK, :]

    def h_copy(d, i):
        if i < 2:
            b, tile = i, x
        else:
            b, tile = d, (x + NX - 1) % NX if d == 0 else (x + 1) % NX
        to = (x + 1) % NX if d == 0 else (x + NX - 1) % NX
        at = piece(c, tile, b)
        return remote(at, at, hss.at[d, i], hrs.at[d, i], (z * NX + to, t))

    def h_pair(i, b):
        at = piece(c, (x + i) % NX, b)
        return remote(at, at, hps.at[i, b], hpr.at[i, b], sibling)

    k_in.wait()
    q_in.wait()
    v_in.wait()
    row = lax.broadcasted_iota(jnp.int32, (BLOCK, BLOCK), 0)
    col = lax.broadcasted_iota(jnp.int32, (BLOCK, BLOCK), 1)
    causal = col <= row
    masks = (
        [causal & (col < length0)],
        [col < reach0, causal & (col + shift1 < length1)],
    )
    for b in range(2):
        keys = [kv[j * BLOCK : (j + 1) * BLOCK, :] for j in range(b + 1)]
        values = [vv[j * BLOCK : (j + 1) * BLOCK, :] for j in range(b + 1)]
        for h in range(HEADS):
            query = qv[b * BLOCK : (b + 1) * BLOCK, h * DIM : (h + 1) * DIM]
            scores = [
                jnp.where(mask, matmul_t(query, key), -1e30)
                for mask, key in zip(masks[b], keys)
            ]
            peak = functools.reduce(
                jnp.maximum, [jnp.max(s, axis=1, keepdims=True) for s in scores]
            )
            expo = [jnp.exp2((s - peak) * EXP2_SCALE) for s in scores]
            total = functools.reduce(
                jnp.add, [jnp.sum(e, axis=1, keepdims=True) for e in expo]
            )
            inverse = 1.0 / total
            mixed = functools.reduce(
                jnp.add,
                [matmul((e * inverse).astype(BF16), value) for e, value in zip(expo, values)],
            )
            hbuf[c, x, b * BLOCK : (b + 1) * BLOCK, h * DIM : (h + 1) * DIM] = mixed.astype(BF16)
        for d in range(2):
            h_copy(d, b).start()
        h_pair(0, b).start()
    w_pair.start()
    p_pair.start()
    for d in range(1, NX):
        slot_copy(d).start()

    def h_arrived(d, i):
        h_copy(d, i).wait_recv()
        if (d, i) in ((0, 0), (1, 1)):
            h_copy(d, 2).start()
        at, b = ((3, i), (1, i))[d] if i < 2 else (2, d)
        h_pair(at, b).start()

    w_arrived(1)
    p_arrived(1)
    h_arrived(0, 0)
    h_arrived(1, 0)
    p_arrived(2)
    w_arrived(2)
    p_arrived(3)
    h_arrived(1, 1)
    h_arrived(0, 1)
    p_arrived(4)
    w_arrived(3)
    p_arrived(5)
    h_arrived(0, 2)
    h_arrived(1, 2)
    w_in.wait()
    d_in.wait()
    up_in.wait()
    w_pair.wait_recv()
    p_pair.wait_recv()
    for d in range(1, NX):
        slot_copy(d).wait_recv()
    for i in (0, 3, 1, 2):
        for b in range(2):
            h_pair(i, b).wait_recv()

    near = (y + 1 - 2 * (y % 2), NY - 1 - y)
    first = near[0] * (1 - c) + near[1] * c
    second = near[1] * (1 - c) + near[0] * c

    def set_of(n, at):
        return (x + (1 + 2 * c) * (at + n)) % NX

    def half_copy(n):
        k, count = GROUPS[n]
        return remote(
            hsend.at[k : k + count], hrec.at[k : k + count], hfs.at[n], hfr.at[n],
            (g, 2 * first + c),
        )

    def quarter_copy(n):
        k, count = GROUPS[n]
        return remote(
            qsend.at[k : k + count], qrec.at[k : k + count], qfs.at[n], qfr.at[n],
            (g, 2 * second + c),
        )

    def multiply(n):
        k, count = GROUPS[n]
        weights = [
            jnp.concatenate([wbuf[k + i, core] for i in range(count)], axis=1)
            for core in range(2)
        ]

        def rows(at, dst, i):
            at = set_of(n, at)
            value = matmul(hbuf[0, at], weights[0]) + matmul(hbuf[1, at], weights[1])
            for j in range(count):
                dst[k + j, i] = value[:, j * 128 : (j + 1) * 128].astype(BF16)

        rows(first, hsend, 0)
        rows((y + 2) % NY, hsend, 1)
        half_copy(n).start()
        rows(second, kept, 1)
        rows(y, kept, 0)

    def quarter(n):
        k, count = GROUPS[n]
        half_copy(n).wait_recv()
        for j in range(k, k + count):
            qsend[j] = (kept[j, 1].astype(F32) + hrec[j, 1].astype(F32)).astype(BF16)
        quarter_copy(n).start()

    def fin_copy(n):
        k, count = GROUPS[n]
        tile, half = place(k, c)
        dst = fin.at[x] if count == 2 else fin.at[x, pl.ds(half, 1)]
        return remote(
            fsend.at[k : k + count], dst, fss.at[n], frs.at[n, x, c],
            (z * NX + set_of(n, y), tile),
        )

    def stays(n):
        return (set_of(n, y) == x) & (place(GROUPS[n][0], c)[0] == t)

    def finish(n):
        k, count = GROUPS[n]
        quarter_copy(n).wait_recv()
        for j in range(k, k + count):
            value = (
                kept[j, 0].astype(F32) + hrec[j, 0].astype(F32) + qrec[j].astype(F32)
            ).astype(BF16)
            half = place(j, c)[1]
            fsend[k + half if count == 2 else k] = value

            @pl.when(stays(n))
            def _():
                fin[x, half] = value

        @pl.when(jnp.logical_not(stays(n)))
        def _():
            fin_copy(n).start()

    def shrink_copy(d):
        return remote(
            asend.at[(x + d) % NX], arec.at[d - 1], axs.at[d - 1], axr.at[d - 1],
            (z * NX + (x + d) % NX, t),
        )

    def tensor_copy(d):
        return remote(tsend, trec.at[d - 1], ats.at[d - 1], atr.at[d - 1], (g, (t + d) % NT))

    def shrink():
        pages = [pbuf[:, core].reshape(NZ * 32, WIDTH) for core in range(2)]
        lane = lax.broadcasted_iota(jnp.int32, (1, NZ * 32), 1)
        page = (place(lane // 32, c)[0] * NX + x).astype(F32)
        at = lax.broadcasted_iota(jnp.int32, (NZ * 32, 128), 0)
        at = at % 32 + 32 * place(at // 32, c)[1]
        to = lax.broadcasted_iota(jnp.int32, (NZ * 32, 128), 1)
        for i in range(NX):
            total = jnp.zeros((BLOCK, 128), F32)
            value = matmul_t(hbuf[0, i], pages[0]) + matmul_t(hbuf[1, i], pages[1])
            for b in range(2):
                slot = jnp.concatenate([slots[i, b : b + 1, :]] * (NZ * 32 // 128), axis=1)
                rows = jnp.where(slot == page, value[b * BLOCK : (b + 1) * BLOCK, :], 0.0)
                total = total + matmul(rows.astype(BF16), (to == at + 64 * b).astype(BF16))
            asend[i] = total.astype(BF16)
        for d in range(1, NX):
            shrink_copy(d).start()

    def shrink_x():
        total = asend[x].astype(F32)
        for d in range(1, NX):
            shrink_copy(d).wait_recv()
            total = total + arec[d - 1].astype(F32)
        tsend[...] = total.astype(BF16)
        for d in range(1, NT):
            tensor_copy(d).start()

    def expand():
        total = tsend[...].astype(F32)
        for d in range(1, NT):
            tensor_copy(d).wait_recv()
            total = total + trec[d - 1].astype(F32)
        shrunk = total.astype(BF16)
        lane = lax.broadcasted_iota(jnp.int32, (BLOCK, 128), 1)
        for b, slot in enumerate((slot0, slot1)):
            acc[b * BLOCK : (b + 1) * BLOCK, :] = matmul(
                jnp.where(lane // 64 == b, shrunk, jnp.zeros_like(shrunk)),
                jnp.concatenate([upv[slot], upv[slot]], axis=0),
            )

    stages = {
        "m": multiply, "q": quarter, "f": finish, "w": w_arrived, "p": p_arrived,
        "s": lambda _: shrink(), "x": lambda _: shrink_x(), "e": lambda _: expand(),
    }
    for stage in ORDER:
        stages[stage[0]](int(stage[1]))

    for s in range(2):
        for core in range(2):
            w_first(core, s).wait_send()
            p_first(core, s).wait_send()

    def sent(s, carry):
        w_copy(s).wait_send()
        p_copy(s).wait_send()
        return carry

    lax.fori_loop(2, LAST, sent, 0)
    w_pair.wait_send()
    p_pair.wait_send()
    for d in range(2):
        for i in range(3):
            h_copy(d, i).wait_send()
    for i in range(NX):
        for b in range(2):
            h_pair(i, b).wait_send()
    for d in range(1, NX):
        slot_copy(d).wait_send()
        shrink_copy(d).wait_send()
    for d in range(1, NT):
        tensor_copy(d).wait_send()
    for n in range(len(GROUPS)):
        half_copy(n).wait_send()
        quarter_copy(n).wait_send()

        @pl.when(jnp.logical_not(stays(n)))
        def _():
            fin_copy(n).wait_send()

    for n, (k, count) in enumerate(GROUPS):
        for core in range(2):
            tile, half = place(k, core)

            @pl.when(tile == t)
            def _():
                for i in range(NX):

                    @pl.when(jnp.logical_not(stays(n) & (x == i) & (c == core)))
                    def _():
                        at = fin.at[i, pl.ds(0, count)]
                        remote(at, at, fss.at[0], frs.at[n, i, core], sibling).wait_recv()

    position = lax.broadcasted_iota(jnp.int32, (BLOCK, 128), 0)
    valid = (position < length0, position + shift1 < length1)
    for b in range(2):
        for i in range(NX):
            for half in range(2):
                cols = slice(i * 256 + half * 128, i * 256 + half * 128 + 128)
                base = fin[i, half, b * BLOCK : (b + 1) * BLOCK, :].astype(F32)
                value = base + acc[b * BLOCK : (b + 1) * BLOCK, cols]
                out_ref[b * BLOCK : (b + 1) * BLOCK, cols] = jnp.where(
                    valid[b], value, 0.0
                ).astype(BF16)


def per_device(q, k, v, w, down, up, tenants, page_slots, lengths):
    dma = pltpu.SemaphoreType.DMA
    anywhere = pl.BlockSpec(memory_space=pl.ANY)
    scalars = pl.BlockSpec(memory_space=pltpu.SMEM)
    rows = 2 * BLOCK
    groups = len(GROUPS)
    return pl.pallas_call(
        kernel,
        out_shape=jax.ShapeDtypeStruct((rows, WIDTH), BF16),
        in_specs=[anywhere] * 6 + [scalars] * 3,
        out_specs=pl.BlockSpec(memory_space=pltpu.VMEM),
        scratch_shapes=[
            pltpu.VMEM((rows, WIDTH), BF16),
            pltpu.VMEM((rows, DIM), BF16),
            pltpu.VMEM((rows, DIM), BF16),
            pltpu.VMEM((2, NX, rows, WIDTH), BF16),
            pltpu.VMEM((NX, 8, 128), F32),
            pltpu.VMEM((NZ, 2, WIDTH, 128), BF16),
            pltpu.VMEM((NZ, 2, 32, WIDTH), BF16),
            pltpu.VMEM((32, 64, WIDTH), BF16),
            pltpu.VMEM((NZ, 2, rows, 128), BF16),
            pltpu.VMEM((NZ, 2, rows, 128), BF16),
            pltpu.VMEM((NZ, 2, rows, 128), BF16),
            pltpu.VMEM((NZ, rows, 128), BF16),
            pltpu.VMEM((NZ, rows, 128), BF16),
            pltpu.VMEM((NZ, rows, 128), BF16),
            pltpu.VMEM((NX, 2, rows, 128), BF16),
            pltpu.VMEM((rows, WIDTH), F32),
            pltpu.VMEM((NX, BLOCK, 128), BF16),
            pltpu.VMEM((NX - 1, BLOCK, 128), BF16),
            pltpu.VMEM((BLOCK, 128), BF16),
            pltpu.VMEM((NT - 1, BLOCK, 128), BF16),
            dma((6,)),
            dma((2, 2)), dma((2, 2)), dma((LAST,)), dma((LAST,)),
            dma((2, 2)), dma((2, 2)), dma((LAST,)), dma((LAST,)),
            dma((2,)), dma((2,)),
            dma((2, 3)), dma((2, 3)), dma((NX, 2)), dma((NX, 2)),
            dma((NX - 1,)), dma((NX - 1,)),
            dma((groups,)), dma((groups,)), dma((groups,)), dma((groups,)),
            dma((groups,)), dma((groups, NX, 2)),
            dma((NX - 1,)), dma((NX - 1,)),
            dma((NT - 1,)), dma((NT - 1,)),
        ],
        compiler_params=pltpu.CompilerParams(
            collective_id=0, has_side_effects=True, vmem_limit_bytes=56 << 20
        ),
    )(q, k, v, w, jnp.swapaxes(down[0], 0, 1), up, tenants, page_slots, lengths)


def solution(mesh):
    placed = (
        P("group", "tensor"),
        P("group", "tensor"),
        P("group", "tensor"),
        P("tensor", "group"),
        P("group", "tensor", None),
        P(None, None, "tensor"),
        P("group"),
        P(),
        P(),
    )
    return jax.shard_map(
        per_device, mesh=mesh, in_specs=placed, out_specs=P("group", "tensor"), check_vma=False
    )
```

```python
import functools

import jax
import jax.numpy as jnp
from jax import lax
from jax.experimental import pallas as pl
from jax.experimental.pallas import tpu as pltpu
from jax.sharding import PartitionSpec as P

MESH = pl.DeviceIdType.MESH
HEADS = 8
DIM = 128
BLOCK = 128
NZ, NX, NY, NT = 8, 4, 4, 8
WIDTH = 1024
LAST = 7
GROUPS = ((0, 1), (1, 2), (3, 2), (5, 1), (6, 1), (7, 1))
ORDER = (
    "m0", "m1", "q0", "w4", "m2", "q1", "f0", "w5", "m3", "q2", "f1", "p6",
    "p7", "w6", "m4", "q3", "f2", "f3", "q4", "s0", "w7", "m5", "f4", "x0",
    "q5", "e0", "f5",
)
EXP2_SCALE = DIM ** (-0.5) * 1.4426950408889634
F32 = jnp.float32
BF16 = jnp.bfloat16


def matmul(a, b):
    return jnp.dot(a, b, preferred_element_type=F32)


def matmul_t(a, b):
    return lax.dot_general(a, b, (((1,), (1,)), ((), ())), preferred_element_type=F32)


def kernel(
    q_hbm, k_hbm, v_hbm, w_hbm, down_hbm, up_hbm, tenant_ref, slot_ref, length_ref,
    out_ref,
    qv, kv, vv, hbuf, slots, wbuf, pbuf, upv,
    kept, hsend, hrec, qsend, qrec, fsend, fin, acc,
    asend, arec, tsend, trec,
    lsem, wfs, wfr, wss, wrs, pfs, pfr, pss, prs, wps, wpr, hss, hrs, hps, hpr, sss, srs,
    hfs, hfr, qfs, qfr, fss, frs, axs, axr, ats, atr,
):
    g, t = lax.axis_index("group"), lax.axis_index("tensor")
    z, x = g // NX, g % NX
    y, c = t // 2, t % 2
    z_next = ((z + 1) % NZ) * NX + x
    z_prev = ((z + NZ - 1) % NZ) * NX + x
    sibling = (g, 2 * y + 1 - c)
    onward = (z_next * (1 - c) + z_prev * c, t)

    barrier = pltpu.get_barrier_semaphore()
    for peer in (z_next, z_prev):
        for core in range(2):
            pl.semaphore_signal(
                barrier, inc=1, device_id=(peer, 2 * y + core), device_id_type=MESH
            )

    def greet(d, carry):
        peer = (x * NT + t + d) % (NX * NT)
        pl.semaphore_signal(
            barrier, inc=1, device_id=(z * NX + peer // NT, peer % NT), device_id_type=MESH
        )
        return carry

    lax.fori_loop(1, NX * NT, greet, 0)
    pl.semaphore_wait(barrier, NX * NT + 3)

    def remote(src, dst, ssem, rsem, device):
        return pltpu.make_async_remote_copy(
            src_ref=src, dst_ref=dst, send_sem=ssem, recv_sem=rsem,
            device_id=device, device_id_type=MESH,
        )

    def place(k, core):
        off = (k + 1) // 2
        return (z + off * (NZ - 1 + 2 * core)) % NZ, ((k + 1) % 2 + core) % 2

    def w_first(core, s):
        half = s % 2 if core == 0 else 1 - s % 2
        return remote(
            w_hbm.at[:, half * 128 : half * 128 + 128], wbuf.at[s + 1, c],
            wfs.at[core, s], wfr.at[s, c], (z_next if core == 0 else z_prev, 2 * y + core),
        )

    def p_first(core, s):
        half = s % 2 if core == 0 else 1 - s % 2
        return remote(
            down_hbm.at[half * 32 : half * 32 + 32, :], pbuf.at[s + 1, c],
            pfs.at[core, s], pfr.at[s, c], (z_next if core == 0 else z_prev, 2 * y + core),
        )

    def w_copy(s):
        return remote(wbuf.at[s - 1], wbuf.at[s + 1], wss.at[s], wrs.at[s], onward)

    def p_copy(s):
        return remote(pbuf.at[s - 1], pbuf.at[s + 1], pss.at[s], prs.at[s], onward)

    for s in range(2):
        for make in (p_first, w_first):
            for core in range(2):
                make(core, s).start()

    def arrived(buf, fr, make, j):
        if j <= 2:
            for core in range(2):
                at = buf.at[j, core]
                remote(at, at, wss.at[0], fr.at[j - 1, core], onward).wait_recv()
        else:
            make(j - 1).wait_recv()
        if j + 1 < LAST:
            make(j + 1).start()

    w_arrived = functools.partial(arrived, wbuf, wfr, w_copy)
    p_arrived = functools.partial(arrived, pbuf, pfr, p_copy)

    def halves(ref, at):
        return ref.at[:, pl.ds(pl.multiple_of(at * 128, 128), 128)]

    w_pair = remote(halves(w_hbm, c), wbuf.at[0, c], wps.at[0], wpr.at[0], sibling)
    p_pair = remote(
        down_hbm.at[pl.ds(pl.multiple_of(c * 32, 32), 32), :], pbuf.at[0, c],
        wps.at[1], wpr.at[1], sibling,
    )
    q_in = pltpu.make_async_copy(q_hbm, qv, lsem.at[0])
    k_in = pltpu.make_async_copy(k_hbm, kv, lsem.at[1])
    v_in = pltpu.make_async_copy(v_hbm, vv, lsem.at[2])
    w_in = pltpu.make_async_copy(halves(w_hbm, 1 - c), wbuf.at[0, c], lsem.at[3])
    d_in = pltpu.make_async_copy(
        down_hbm.at[pl.ds(pl.multiple_of((1 - c) * 32, 32), 32), :], pbuf.at[0, c], lsem.at[4]
    )
    up_in = pltpu.make_async_copy(up_hbm, upv, lsem.at[5])
    for copy in (k_in, q_in, v_in, w_in, d_in, up_in):
        copy.start()

    tenant0, tenant1 = tenant_ref[0], tenant_ref[1]
    same = tenant0 == tenant1
    length0, length1 = length_ref[tenant0], length_ref[tenant1]
    slot0, slot1 = slot_ref[tenant0], slot_ref[tenant1]
    shift1 = jnp.where(same, BLOCK, 0)
    reach0 = jnp.where(same, length0, 0)

    rows8 = lax.broadcasted_iota(jnp.int32, (8, 128), 0)
    slots[x] = jnp.where(rows8 == 0, slot0, slot1).astype(F32)

    def slot_copy(d):
        return remote(
            slots.at[x], slots.at[x], sss.at[d - 1], srs.at[d - 1], (z * NX + (x + d) % NX, t)
        )

    def piece(core, tile, b):
        return hbuf.at[core, tile, b * BLOCK : (b + 1) * BLOCK, :]

    def h_copy(d, i):
        if i < 2:
            b, tile = i, x
        else:
            b, tile = d, (x + NX - 1) % NX if d == 0 else (x + 1) % NX
        to = (x + 1) % NX if d == 0 else (x + NX - 1) % NX
        at = piece(c, tile, b)
        return remote(at, at, hss.at[d, i], hrs.at[d, i], (z * NX + to, t))

    def h_pair(i, b):
        at = piece(c, (x + i) % NX, b)
        return remote(at, at, hps.at[i, b], hpr.at[i, b], sibling)

    k_in.wait()
    q_in.wait()
    v_in.wait()
    row = lax.broadcasted_iota(jnp.int32, (BLOCK, BLOCK), 0)
    col = lax.broadcasted_iota(jnp.int32, (BLOCK, BLOCK), 1)
    causal = col <= row
    masks = (
        [causal & (col < length0)],
        [col < reach0, causal & (col + shift1 < length1)],
    )
    for b in range(2):
        keys = [kv[j * BLOCK : (j + 1) * BLOCK, :] for j in range(b + 1)]
        values = [vv[j * BLOCK : (j + 1) * BLOCK, :] for j in range(b + 1)]
        for h in range(HEADS):
            query = qv[b * BLOCK : (b + 1) * BLOCK, h * DIM : (h + 1) * DIM]
            scores = [
                jnp.where(mask, matmul_t(query, key), -1e30)
                for mask, key in zip(masks[b], keys)
            ]
            peak = functools.reduce(
                jnp.maximum, [jnp.max(s, axis=1, keepdims=True) for s in scores]
            )
            expo = [jnp.exp2((s - peak) * EXP2_SCALE) for s in scores]
            total = functools.reduce(
                jnp.add, [jnp.sum(e, axis=1, keepdims=True) for e in expo]
            )
            inverse = 1.0 / total
            mixed = functools.reduce(
                jnp.add,
                [matmul((e * inverse).astype(BF16), value) for e, value in zip(expo, values)],
            )
            hbuf[c, x, b * BLOCK : (b + 1) * BLOCK, h * DIM : (h + 1) * DIM] = mixed.astype(BF16)
        for d in range(2):
            h_copy(d, b).start()
        h_pair(0, b).start()
    w_pair.start()
    p_pair.start()
    for d in range(1, NX):
        slot_copy(d).start()

    def h_arrived(d, i):
        h_copy(d, i).wait_recv()
        if (d, i) in ((0, 0), (1, 1)):
            h_copy(d, 2).start()
        at, b = ((3, i), (1, i))[d] if i < 2 else (2, d)
        h_pair(at, b).start()

    w_arrived(1)
    p_arrived(1)
    h_arrived(0, 0)
    h_arrived(1, 0)
    p_arrived(2)
    w_arrived(2)
    p_arrived(3)
    h_arrived(1, 1)
    h_arrived(0, 1)
    p_arrived(4)
    w_arrived(3)
    p_arrived(5)
    h_arrived(0, 2)
    h_arrived(1, 2)
    w_in.wait()
    d_in.wait()
    up_in.wait()
    w_pair.wait_recv()
    p_pair.wait_recv()
    for d in range(1, NX):
        slot_copy(d).wait_recv()
    for i in (0, 3, 1, 2):
        for b in range(2):
            h_pair(i, b).wait_recv()

    near = (y + 1 - 2 * (y % 2), NY - 1 - y)
    first = near[0] * (1 - c) + near[1] * c
    second = near[1] * (1 - c) + near[0] * c

    def set_of(n, at):
        return (x + (1 + 2 * c) * (at + n)) % NX

    def half_copy(n):
        k, count = GROUPS[n]
        return remote(
            hsend.at[k : k + count], hrec.at[k : k + count], hfs.at[n], hfr.at[n],
            (g, 2 * first + c),
        )

    def quarter_copy(n):
        k, count = GROUPS[n]
        return remote(
            qsend.at[k : k + count], qrec.at[k : k + count], qfs.at[n], qfr.at[n],
            (g, 2 * second + c),
        )

    def multiply(n):
        k, count = GROUPS[n]
        weights = [
            jnp.concatenate([wbuf[k + i, core] for i in range(count)], axis=1)
            for core in range(2)
        ]

        def rows(at, dst, i):
            at = set_of(n, at)
            value = matmul(hbuf[0, at], weights[0]) + matmul(hbuf[1, at], weights[1])
            for j in range(count):
                dst[k + j, i] = value[:, j * 128 : (j + 1) * 128].astype(BF16)

        rows(first, hsend, 0)
        rows((y + 2) % NY, hsend, 1)
        half_copy(n).start()
        rows(second, kept, 1)
        rows(y, kept, 0)

    def quarter(n):
        k, count = GROUPS[n]
        half_copy(n).wait_recv()
        for j in range(k, k + count):
            qsend[j] = (kept[j, 1].astype(F32) + hrec[j, 1].astype(F32)).astype(BF16)
        quarter_copy(n).start()

    def fin_copy(n):
        k, count = GROUPS[n]
        tile, half = place(k, c)
        dst = fin.at[x] if count == 2 else fin.at[x, pl.ds(half, 1)]
        return remote(
            fsend.at[k : k + count], dst, fss.at[n], frs.at[n, x, c],
            (z * NX + set_of(n, y), tile),
        )

    def stays(n):
        return (set_of(n, y) == x) & (place(GROUPS[n][0], c)[0] == t)

    def finish(n):
        k, count = GROUPS[n]
        quarter_copy(n).wait_recv()
        for j in range(k, k + count):
            value = (
                kept[j, 0].astype(F32) + hrec[j, 0].astype(F32) + qrec[j].astype(F32)
            ).astype(BF16)
            half = place(j, c)[1]
            fsend[k + half if count == 2 else k] = value

            @pl.when(stays(n))
            def _():
                fin[x, half] = value

        @pl.when(jnp.logical_not(stays(n)))
        def _():
            fin_copy(n).start()

    def shrink_copy(d):
        return remote(
            asend.at[(x + d) % NX], arec.at[d - 1], axs.at[d - 1], axr.at[d - 1],
            (z * NX + (x + d) % NX, t),
        )

    def tensor_copy(d):
        return remote(tsend, trec.at[d - 1], ats.at[d - 1], atr.at[d - 1], (g, (t + d) % NT))

    def shrink():
        pages = [pbuf[:, core].reshape(NZ * 32, WIDTH) for core in range(2)]
        lane = lax.broadcasted_iota(jnp.int32, (1, NZ * 32), 1)
        page = (place(lane // 32, c)[0] * NX + x).astype(F32)
        at = lax.broadcasted_iota(jnp.int32, (NZ * 32, 128), 0)
        at = at % 32 + 32 * place(at // 32, c)[1]
        to = lax.broadcasted_iota(jnp.int32, (NZ * 32, 128), 1)
        for i in range(NX):
            total = jnp.zeros((BLOCK, 128), F32)
            value = matmul_t(hbuf[0, i], pages[0]) + matmul_t(hbuf[1, i], pages[1])
            for b in range(2):
                slot = jnp.concatenate([slots[i, b : b + 1, :]] * (NZ * 32 // 128), axis=1)
                rows = jnp.where(slot == page, value[b * BLOCK : (b + 1) * BLOCK, :], 0.0)
                total = total + matmul(rows.astype(BF16), (to == at + 64 * b).astype(BF16))
            asend[i] = total.astype(BF16)
        for d in range(1, NX):
            shrink_copy(d).start()

    def shrink_x():
        total = asend[x].astype(F32)
        for d in range(1, NX):
            shrink_copy(d).wait_recv()
            total = total + arec[d - 1].astype(F32)
        tsend[...] = total.astype(BF16)
        for d in range(1, NT):
            tensor_copy(d).start()

    def expand():
        total = tsend[...].astype(F32)
        for d in range(1, NT):
            tensor_copy(d).wait_recv()
            total = total + trec[d - 1].astype(F32)
        shrunk = total.astype(BF16)
        lane = lax.broadcasted_iota(jnp.int32, (BLOCK, 128), 1)
        for b, slot in enumerate((slot0, slot1)):
            acc[b * BLOCK : (b + 1) * BLOCK, :] = matmul(
                jnp.where(lane // 64 == b, shrunk, jnp.zeros_like(shrunk)),
                jnp.concatenate([upv[slot], upv[slot]], axis=0),
            )

    stages = {
        "m": multiply, "q": quarter, "f": finish, "w": w_arrived, "p": p_arrived,
        "s": lambda _: shrink(), "x": lambda _: shrink_x(), "e": lambda _: expand(),
    }
    for stage in ORDER:
        stages[stage[0]](int(stage[1]))

    for s in range(2):
        for core in range(2):
            w_first(core, s).wait_send()
            p_first(core, s).wait_send()

    def sent(s, carry):
        w_copy(s).wait_send()
        p_copy(s).wait_send()
        return carry

    lax.fori_loop(2, LAST, sent, 0)
    w_pair.wait_send()
    p_pair.wait_send()
    for d in range(2):
        for i in range(3):
            h_copy(d, i).wait_send()
    for i in range(NX):
        for b in range(2):
            h_pair(i, b).wait_send()
    for d in range(1, NX):
        slot_copy(d).wait_send()
        shrink_copy(d).wait_send()
    for d in range(1, NT):
        tensor_copy(d).wait_send()
    for n in range(len(GROUPS)):
        half_copy(n).wait_send()
        quarter_copy(n).wait_send()

        @pl.when(jnp.logical_not(stays(n)))
        def _():
            fin_copy(n).wait_send()

    for n, (k, count) in enumerate(GROUPS):
        for core in range(2):
            tile, half = place(k, core)

            @pl.when(tile == t)
            def _():
                for i in range(NX):

                    @pl.when(jnp.logical_not(stays(n) & (x == i) & (c == core)))
                    def _():
                        at = fin.at[i, pl.ds(0, count)]
                        remote(at, at, fss.at[0], frs.at[n, i, core], sibling).wait_recv()

    position = lax.broadcasted_iota(jnp.int32, (BLOCK, 128), 0)
    valid = (position < length0, position + shift1 < length1)
    for b in range(2):
        for i in range(NX):
            for half in range(2):
                cols = slice(i * 256 + half * 128, i * 256 + half * 128 + 128)
                base = fin[i, half, b * BLOCK : (b + 1) * BLOCK, :].astype(F32)
                value = base + acc[b * BLOCK : (b + 1) * BLOCK, cols]
                out_ref[b * BLOCK : (b + 1) * BLOCK, cols] = jnp.where(
                    valid[b], value, 0.0
                ).astype(BF16)


def per_device(q, k, v, w, down, up, tenants, page_slots, lengths):
    dma = pltpu.SemaphoreType.DMA
    anywhere = pl.BlockSpec(memory_space=pl.ANY)
    scalars = pl.BlockSpec(memory_space=pltpu.SMEM)
    rows = 2 * BLOCK
    groups = len(GROUPS)
    return pl.pallas_call(
        kernel,
        out_shape=jax.ShapeDtypeStruct((rows, WIDTH), BF16),
        in_specs=[anywhere] * 6 + [scalars] * 3,
        out_specs=pl.BlockSpec(memory_space=pltpu.VMEM),
        scratch_shapes=[
            pltpu.VMEM((rows, WIDTH), BF16),
            pltpu.VMEM((rows, DIM), BF16),
            pltpu.VMEM((rows, DIM), BF16),
            pltpu.VMEM((2, NX, rows, WIDTH), BF16),
            pltpu.VMEM((NX, 8, 128), F32),
            pltpu.VMEM((NZ, 2, WIDTH, 128), BF16),
            pltpu.VMEM((NZ, 2, 32, WIDTH), BF16),
            pltpu.VMEM((32, 64, WIDTH), BF16),
            pltpu.VMEM((NZ, 2, rows, 128), BF16),
            pltpu.VMEM((NZ, 2, rows, 128), BF16),
            pltpu.VMEM((NZ, 2, rows, 128), BF16),
            pltpu.VMEM((NZ, rows, 128), BF16),
            pltpu.VMEM((NZ, rows, 128), BF16),
            pltpu.VMEM((NZ, rows, 128), BF16),
            pltpu.VMEM((NX, 2, rows, 128), BF16),
            pltpu.VMEM((rows, WIDTH), F32),
            pltpu.VMEM((NX, BLOCK, 128), BF16),
            pltpu.VMEM((NX - 1, BLOCK, 128), BF16),
            pltpu.VMEM((BLOCK, 128), BF16),
            pltpu.VMEM((NT - 1, BLOCK, 128), BF16),
            dma((6,)),
            dma((2, 2)), dma((2, 2)), dma((LAST,)), dma((LAST,)),
            dma((2, 2)), dma((2, 2)), dma((LAST,)), dma((LAST,)),
            dma((2,)), dma((2,)),
            dma((2, 3)), dma((2, 3)), dma((NX, 2)), dma((NX, 2)),
            dma((NX - 1,)), dma((NX - 1,)),
            dma((groups,)), dma((groups,)), dma((groups,)), dma((groups,)),
            dma((groups,)), dma((groups, NX, 2)),
            dma((NX - 1,)), dma((NX - 1,)),
            dma((NT - 1,)), dma((NT - 1,)),
        ],
        compiler_params=pltpu.CompilerParams(
            collective_id=0, has_side_effects=True, vmem_limit_bytes=56 << 20
        ),
    )(q, k, v, w, jnp.swapaxes(down[0], 0, 1), up, tenants, page_slots, lengths)


def solution(mesh):
    placed = (
        P("group", "tensor"),
        P("group", "tensor"),
        P("group", "tensor"),
        P("tensor", "group"),
        P("group", "tensor", None),
        P(None, None, "tensor"),
        P("group"),
        P(),
        P(),
    )
    return jax.shard_map(
        per_device, mesh=mesh, in_specs=placed, out_specs=P("group", "tensor"), check_vma=False
    )
```

```python
import functools

import jax
import jax.numpy as jnp
from jax import lax
from jax.experimental import pallas as pl
from jax.experimental.pallas import tpu as pltpu
from jax.sharding import PartitionSpec as P

MESH = pl.DeviceIdType.MESH
HEADS = 8
DIM = 128
BLOCK = 128
NZ, NX, NY, NT = 8, 4, 4, 8
WIDTH = 1024
LAST = 7
GROUPS = ((0, 1), (1, 2), (3, 2), (5, 1), (6, 1), (7, 1))
ORDER = (
    "m0", "m1", "q0", "w4", "m2", "q1", "f0", "w5", "m3", "q2", "f1", "p6",
    "p7", "w6", "m4", "q3", "f2", "f3", "q4", "s0", "w7", "m5", "f4", "x0",
    "q5", "e0", "f5",
)
EXP2_SCALE = DIM ** (-0.5) * 1.4426950408889634
F32 = jnp.float32
BF16 = jnp.bfloat16


def matmul(a, b):
    return jnp.dot(a, b, preferred_element_type=F32)


def matmul_t(a, b):
    return lax.dot_general(a, b, (((1,), (1,)), ((), ())), preferred_element_type=F32)


def kernel(
    q_hbm, k_hbm, v_hbm, w_hbm, down_hbm, up_hbm, tenant_ref, slot_ref, length_ref,
    out_ref,
    qv, kv, vv, hbuf, slots, wbuf, pbuf, upv,
    kept, hsend, hrec, qsend, qrec, fsend, fin, acc,
    asend, arec, tsend, trec,
    lsem, wfs, wfr, wss, wrs, pfs, pfr, pss, prs, wps, wpr, hss, hrs, hps, hpr, sss, srs,
    hfs, hfr, qfs, qfr, fss, frs, axs, axr, ats, atr,
):
    g, t = lax.axis_index("group"), lax.axis_index("tensor")
    z, x = g // NX, g % NX
    y, c = t // 2, t % 2
    z_next = ((z + 1) % NZ) * NX + x
    z_prev = ((z + NZ - 1) % NZ) * NX + x
    sibling = (g, 2 * y + 1 - c)
    onward = (z_next * (1 - c) + z_prev * c, t)

    q_in = pltpu.make_async_copy(q_hbm, qv, lsem.at[0])
    k_in = pltpu.make_async_copy(k_hbm, kv, lsem.at[1])
    v_in = pltpu.make_async_copy(v_hbm, vv, lsem.at[2])
    for copy in (k_in, q_in, v_in):
        copy.start()

    barrier = pltpu.get_barrier_semaphore()
    for peer in (z_next, z_prev):
        for core in range(2):
            pl.semaphore_signal(
                barrier, inc=1, device_id=(peer, 2 * y + core), device_id_type=MESH
            )

    def greet(d, carry):
        peer = (x * NT + t + d) % (NX * NT)
        pl.semaphore_signal(
            barrier, inc=1, device_id=(z * NX + peer // NT, peer % NT), device_id_type=MESH
        )
        return carry

    lax.fori_loop(1, NX * NT, greet, 0)
    pl.semaphore_wait(barrier, NX * NT + 3)

    def remote(src, dst, ssem, rsem, device):
        return pltpu.make_async_remote_copy(
            src_ref=src, dst_ref=dst, send_sem=ssem, recv_sem=rsem,
            device_id=device, device_id_type=MESH,
        )

    def place(k, core):
        off = (k + 1) // 2
        return (z + off * (NZ - 1 + 2 * core)) % NZ, ((k + 1) % 2 + core) % 2

    def w_first(core, s):
        half = s % 2 if core == 0 else 1 - s % 2
        return remote(
            w_hbm.at[:, half * 128 : half * 128 + 128], wbuf.at[s + 1, c],
            wfs.at[core, s], wfr.at[s, c], (z_next if core == 0 else z_prev, 2 * y + core),
        )

    def p_first(core, s):
        half = s % 2 if core == 0 else 1 - s % 2
        return remote(
            down_hbm.at[half * 32 : half * 32 + 32, :], pbuf.at[s + 1, c],
            pfs.at[core, s], pfr.at[s, c], (z_next if core == 0 else z_prev, 2 * y + core),
        )

    def w_copy(s):
        return remote(wbuf.at[s - 1], wbuf.at[s + 1], wss.at[s], wrs.at[s], onward)

    def p_copy(s):
        return remote(pbuf.at[s - 1], pbuf.at[s + 1], pss.at[s], prs.at[s], onward)

    for s in range(2):
        for make in (p_first, w_first):
            for core in range(2):
                make(core, s).start()

    def arrived(buf, fr, make, j):
        if j <= 2:
            for core in range(2):
                at = buf.at[j, core]
                remote(at, at, wss.at[0], fr.at[j - 1, core], onward).wait_recv()
        else:
            make(j - 1).wait_recv()
        if j + 1 < LAST:
            make(j + 1).start()

    w_arrived = functools.partial(arrived, wbuf, wfr, w_copy)
    p_arrived = functools.partial(arrived, pbuf, pfr, p_copy)

    def halves(ref, at):
        return ref.at[:, pl.ds(pl.multiple_of(at * 128, 128), 128)]

    w_pair = remote(halves(w_hbm, c), wbuf.at[0, c], wps.at[0], wpr.at[0], sibling)
    p_pair = remote(
        down_hbm.at[pl.ds(pl.multiple_of(c * 32, 32), 32), :], pbuf.at[0, c],
        wps.at[1], wpr.at[1], sibling,
    )
    w_in = pltpu.make_async_copy(halves(w_hbm, 1 - c), wbuf.at[0, c], lsem.at[3])
    d_in = pltpu.make_async_copy(
        down_hbm.at[pl.ds(pl.multiple_of((1 - c) * 32, 32), 32), :], pbuf.at[0, c], lsem.at[4]
    )
    up_in = pltpu.make_async_copy(up_hbm, upv, lsem.at[5])
    for copy in (w_in, d_in, up_in):
        copy.start()

    tenant0, tenant1 = tenant_ref[0], tenant_ref[1]
    same = tenant0 == tenant1
    length0, length1 = length_ref[tenant0], length_ref[tenant1]
    slot0, slot1 = slot_ref[tenant0], slot_ref[tenant1]
    shift1 = jnp.where(same, BLOCK, 0)
    reach0 = jnp.where(same, length0, 0)

    rows8 = lax.broadcasted_iota(jnp.int32, (8, 128), 0)
    slots[x] = jnp.where(rows8 == 0, slot0, slot1).astype(F32)

    def slot_copy(d):
        return remote(
            slots.at[x], slots.at[x], sss.at[d - 1], srs.at[d - 1], (z * NX + (x + d) % NX, t)
        )

    def piece(core, tile, b):
        return hbuf.at[core, tile, b * BLOCK : (b + 1) * BLOCK, :]

    def h_copy(d, i):
        if i < 2:
            b, tile = i, x
        else:
            b, tile = d, (x + NX - 1) % NX if d == 0 else (x + 1) % NX
        to = (x + 1) % NX if d == 0 else (x + NX - 1) % NX
        at = piece(c, tile, b)
        return remote(at, at, hss.at[d, i], hrs.at[d, i], (z * NX + to, t))

    def h_pair(i, b):
        at = piece(c, (x + i) % NX, b)
        return remote(at, at, hps.at[i, b], hpr.at[i, b], sibling)

    k_in.wait()
    q_in.wait()
    v_in.wait()
    row = lax.broadcasted_iota(jnp.int32, (BLOCK, BLOCK), 0)
    col = lax.broadcasted_iota(jnp.int32, (BLOCK, BLOCK), 1)
    causal = col <= row
    masks = (
        [causal & (col < length0)],
        [col < reach0, causal & (col + shift1 < length1)],
    )
    for b in range(2):
        keys = [kv[j * BLOCK : (j + 1) * BLOCK, :] for j in range(b + 1)]
        values = [vv[j * BLOCK : (j + 1) * BLOCK, :] for j in range(b + 1)]
        for h in range(HEADS):
            query = qv[b * BLOCK : (b + 1) * BLOCK, h * DIM : (h + 1) * DIM]
            scores = [
                jnp.where(mask, matmul_t(query, key), -1e30)
                for mask, key in zip(masks[b], keys)
            ]
            peak = functools.reduce(
                jnp.maximum, [jnp.max(s, axis=1, keepdims=True) for s in scores]
            )
            expo = [jnp.exp2((s - peak) * EXP2_SCALE) for s in scores]
            total = functools.reduce(
                jnp.add, [jnp.sum(e, axis=1, keepdims=True) for e in expo]
            )
            inverse = 1.0 / total
            mixed = functools.reduce(
                jnp.add,
                [matmul((e * inverse).astype(BF16), value) for e, value in zip(expo, values)],
            )
            hbuf[c, x, b * BLOCK : (b + 1) * BLOCK, h * DIM : (h + 1) * DIM] = mixed.astype(BF16)
        for d in range(2):
            h_copy(d, b).start()
        h_pair(0, b).start()
    w_pair.start()
    p_pair.start()
    for d in range(1, NX):
        slot_copy(d).start()

    def h_arrived(d, i):
        h_copy(d, i).wait_recv()
        if (d, i) in ((0, 0), (1, 1)):
            h_copy(d, 2).start()
        at, b = ((3, i), (1, i))[d] if i < 2 else (2, d)
        h_pair(at, b).start()

    w_arrived(1)
    p_arrived(1)
    h_arrived(0, 0)
    h_arrived(1, 0)
    p_arrived(2)
    w_arrived(2)
    p_arrived(3)
    h_arrived(1, 1)
    h_arrived(0, 1)
    p_arrived(4)
    w_arrived(3)
    p_arrived(5)
    h_arrived(0, 2)
    h_arrived(1, 2)
    w_in.wait()
    d_in.wait()
    up_in.wait()
    w_pair.wait_recv()
    p_pair.wait_recv()
    for d in range(1, NX):
        slot_copy(d).wait_recv()
    for i in (0, 3, 1, 2):
        for b in range(2):
            h_pair(i, b).wait_recv()

    near = (y + 1 - 2 * (y % 2), NY - 1 - y)
    first = near[0] * (1 - c) + near[1] * c
    second = near[1] * (1 - c) + near[0] * c

    def set_of(n, at):
        return (x + (1 + 2 * c) * (at + n)) % NX

    def half_copy(n):
        k, count = GROUPS[n]
        return remote(
            hsend.at[k : k + count], hrec.at[k : k + count], hfs.at[n], hfr.at[n],
            (g, 2 * first + c),
        )

    def quarter_copy(n):
        k, count = GROUPS[n]
        return remote(
            qsend.at[k : k + count], qrec.at[k : k + count], qfs.at[n], qfr.at[n],
            (g, 2 * second + c),
        )

    def multiply(n):
        k, count = GROUPS[n]
        weights = [
            jnp.concatenate([wbuf[k + i, core] for i in range(count)], axis=1)
            for core in range(2)
        ]

        def rows(at, dst, i):
            at = set_of(n, at)
            value = matmul(hbuf[0, at], weights[0]) + matmul(hbuf[1, at], weights[1])
            for j in range(count):
                dst[k + j, i] = value[:, j * 128 : (j + 1) * 128].astype(BF16)

        rows(first, hsend, 0)
        rows((y + 2) % NY, hsend, 1)
        half_copy(n).start()
        rows(second, kept, 1)
        rows(y, kept, 0)

    def quarter(n):
        k, count = GROUPS[n]
        half_copy(n).wait_recv()
        for j in range(k, k + count):
            qsend[j] = (kept[j, 1].astype(F32) + hrec[j, 1].astype(F32)).astype(BF16)
        quarter_copy(n).start()

    def fin_copy(n):
        k, count = GROUPS[n]
        tile, half = place(k, c)
        dst = fin.at[x] if count == 2 else fin.at[x, pl.ds(half, 1)]
        return remote(
            fsend.at[k : k + count], dst, fss.at[n], frs.at[n, x, c],
            (z * NX + set_of(n, y), tile),
        )

    def stays(n):
        return (set_of(n, y) == x) & (place(GROUPS[n][0], c)[0] == t)

    def finish(n):
        k, count = GROUPS[n]
        quarter_copy(n).wait_recv()
        for j in range(k, k + count):
            value = (
                kept[j, 0].astype(F32) + hrec[j, 0].astype(F32) + qrec[j].astype(F32)
            ).astype(BF16)
            half = place(j, c)[1]
            fsend[k + half if count == 2 else k] = value

            @pl.when(stays(n))
            def _():
                fin[x, half] = value

        @pl.when(jnp.logical_not(stays(n)))
        def _():
            fin_copy(n).start()

    def shrink_copy(d):
        return remote(
            asend.at[(x + d) % NX], arec.at[d - 1], axs.at[d - 1], axr.at[d - 1],
            (z * NX + (x + d) % NX, t),
        )

    def tensor_copy(d):
        return remote(tsend, trec.at[d - 1], ats.at[d - 1], atr.at[d - 1], (g, (t + d) % NT))

    def shrink():
        pages = [pbuf[:, core].reshape(NZ * 32, WIDTH) for core in range(2)]
        lane = lax.broadcasted_iota(jnp.int32, (1, NZ * 32), 1)
        page = (place(lane // 32, c)[0] * NX + x).astype(F32)
        at = lax.broadcasted_iota(jnp.int32, (NZ * 32, 128), 0)
        at = at % 32 + 32 * place(at // 32, c)[1]
        to = lax.broadcasted_iota(jnp.int32, (NZ * 32, 128), 1)
        for i in range(NX):
            total = jnp.zeros((BLOCK, 128), F32)
            value = matmul_t(hbuf[0, i], pages[0]) + matmul_t(hbuf[1, i], pages[1])
            for b in range(2):
                slot = jnp.concatenate([slots[i, b : b + 1, :]] * (NZ * 32 // 128), axis=1)
                rows = jnp.where(slot == page, value[b * BLOCK : (b + 1) * BLOCK, :], 0.0)
                total = total + matmul(rows.astype(BF16), (to == at + 64 * b).astype(BF16))
            asend[i] = total.astype(BF16)
        for d in range(1, NX):
            shrink_copy(d).start()

    def shrink_x():
        total = asend[x].astype(F32)
        for d in range(1, NX):
            shrink_copy(d).wait_recv()
            total = total + arec[d - 1].astype(F32)
        tsend[...] = total.astype(BF16)
        for d in range(1, NT):
            tensor_copy(d).start()

    def expand():
        total = tsend[...].astype(F32)
        for d in range(1, NT):
            tensor_copy(d).wait_recv()
            total = total + trec[d - 1].astype(F32)
        shrunk = total.astype(BF16)
        lane = lax.broadcasted_iota(jnp.int32, (BLOCK, 128), 1)
        for b, slot in enumerate((slot0, slot1)):
            acc[b * BLOCK : (b + 1) * BLOCK, :] = matmul(
                jnp.where(lane // 64 == b, shrunk, jnp.zeros_like(shrunk)),
                jnp.concatenate([upv[slot], upv[slot]], axis=0),
            )

    stages = {
        "m": multiply, "q": quarter, "f": finish, "w": w_arrived, "p": p_arrived,
        "s": lambda _: shrink(), "x": lambda _: shrink_x(), "e": lambda _: expand(),
    }
    for stage in ORDER:
        stages[stage[0]](int(stage[1]))

    for s in range(2):
        for core in range(2):
            w_first(core, s).wait_send()
            p_first(core, s).wait_send()

    def sent(s, carry):
        w_copy(s).wait_send()
        p_copy(s).wait_send()
        return carry

    lax.fori_loop(2, LAST, sent, 0)
    w_pair.wait_send()
    p_pair.wait_send()
    for d in range(2):
        for i in range(3):
            h_copy(d, i).wait_send()
    for i in range(NX):
        for b in range(2):
            h_pair(i, b).wait_send()
    for d in range(1, NX):
        slot_copy(d).wait_send()
        shrink_copy(d).wait_send()
    for d in range(1, NT):
        tensor_copy(d).wait_send()
    for n in range(len(GROUPS)):
        half_copy(n).wait_send()
        quarter_copy(n).wait_send()

        @pl.when(jnp.logical_not(stays(n)))
        def _():
            fin_copy(n).wait_send()

    for n, (k, count) in enumerate(GROUPS):
        for core in range(2):
            tile, half = place(k, core)

            @pl.when(tile == t)
            def _():
                for i in range(NX):

                    @pl.when(jnp.logical_not(stays(n) & (x == i) & (c == core)))
                    def _():
                        at = fin.at[i, pl.ds(0, count)]
                        remote(at, at, fss.at[0], frs.at[n, i, core], sibling).wait_recv()

    position = lax.broadcasted_iota(jnp.int32, (BLOCK, 128), 0)
    valid = (position < length0, position + shift1 < length1)
    for b in range(2):
        for i in range(NX):
            for half in range(2):
                cols = slice(i * 256 + half * 128, i * 256 + half * 128 + 128)
                base = fin[i, half, b * BLOCK : (b + 1) * BLOCK, :].astype(F32)
                value = base + acc[b * BLOCK : (b + 1) * BLOCK, cols]
                out_ref[b * BLOCK : (b + 1) * BLOCK, cols] = jnp.where(
                    valid[b], value, 0.0
                ).astype(BF16)


def per_device(q, k, v, w, down, up, tenants, page_slots, lengths):
    dma = pltpu.SemaphoreType.DMA
    anywhere = pl.BlockSpec(memory_space=pl.ANY)
    scalars = pl.BlockSpec(memory_space=pltpu.SMEM)
    rows = 2 * BLOCK
    groups = len(GROUPS)
    return pl.pallas_call(
        kernel,
        out_shape=jax.ShapeDtypeStruct((rows, WIDTH), BF16),
        in_specs=[anywhere] * 6 + [scalars] * 3,
        out_specs=pl.BlockSpec(memory_space=pltpu.VMEM),
        scratch_shapes=[
            pltpu.VMEM((rows, WIDTH), BF16),
            pltpu.VMEM((rows, DIM), BF16),
            pltpu.VMEM((rows, DIM), BF16),
            pltpu.VMEM((2, NX, rows, WIDTH), BF16),
            pltpu.VMEM((NX, 8, 128), F32),
            pltpu.VMEM((NZ, 2, WIDTH, 128), BF16),
            pltpu.VMEM((NZ, 2, 32, WIDTH), BF16),
            pltpu.VMEM((32, 64, WIDTH), BF16),
            pltpu.VMEM((NZ, 2, rows, 128), BF16),
            pltpu.VMEM((NZ, 2, rows, 128), BF16),
            pltpu.VMEM((NZ, 2, rows, 128), BF16),
            pltpu.VMEM((NZ, rows, 128), BF16),
            pltpu.VMEM((NZ, rows, 128), BF16),
            pltpu.VMEM((NZ, rows, 128), BF16),
            pltpu.VMEM((NX, 2, rows, 128), BF16),
            pltpu.VMEM((rows, WIDTH), F32),
            pltpu.VMEM((NX, BLOCK, 128), BF16),
            pltpu.VMEM((NX - 1, BLOCK, 128), BF16),
            pltpu.VMEM((BLOCK, 128), BF16),
            pltpu.VMEM((NT - 1, BLOCK, 128), BF16),
            dma((6,)),
            dma((2, 2)), dma((2, 2)), dma((LAST,)), dma((LAST,)),
            dma((2, 2)), dma((2, 2)), dma((LAST,)), dma((LAST,)),
            dma((2,)), dma((2,)),
            dma((2, 3)), dma((2, 3)), dma((NX, 2)), dma((NX, 2)),
            dma((NX - 1,)), dma((NX - 1,)),
            dma((groups,)), dma((groups,)), dma((groups,)), dma((groups,)),
            dma((groups,)), dma((groups, NX, 2)),
            dma((NX - 1,)), dma((NX - 1,)),
            dma((NT - 1,)), dma((NT - 1,)),
        ],
        compiler_params=pltpu.CompilerParams(
            collective_id=0, has_side_effects=True, vmem_limit_bytes=56 << 20
        ),
    )(q, k, v, w, jnp.swapaxes(down[0], 0, 1), up, tenants, page_slots, lengths)


def solution(mesh):
    placed = (
        P("group", "tensor"),
        P("group", "tensor"),
        P("group", "tensor"),
        P("tensor", "group"),
        P("group", "tensor", None),
        P(None, None, "tensor"),
        P("group"),
        P(),
        P(),
    )
    return jax.shard_map(
        per_device, mesh=mesh, in_specs=placed, out_specs=P("group", "tensor"), check_vma=False
    )
```
